32 devices in a mesh: row: 4 (over z), col: 8 (over y, x, core).
Axes of the slice: x: 2, y: 2, z: 4, core: 2. Of those that a mesh axis runs over, the one named last changes fastest.
Arguments:
- tokens: bfloat16 [512, 8192], P('row', 'col'), may hold values from -6 to 6
- weight_in: bfloat16 [8192, 32768], P('col', 'row'), may hold values from -0.0625 to 0.0625
- weight_out: bfloat16 [32768, 8192], P('row', 'col'), may hold values from -0.03125 to 0.03125
- upstream: bfloat16 [512, 8192], P('row', 'col'), may hold values from -1.5 to 1.5
Outputs:
- output: bfloat16 [512, 8192], P('row', 'col')
- grad_tokens: bfloat16 [512, 8192], P('row', 'col')
- grad_weight_in: bfloat16 [8192, 32768], P('col', 'row')
- grad_weight_out: bfloat16 [32768, 8192], P('row', 'col')
The draws below stay inside these ranges and needn't reach their ends.
All inputs are finite; a program needn't handle non-finite values.
Results may differ from the reference program's by a relative error of at most 0.0049.
Values may be sent and summed in bfloat16 or wider, within the bound.
A program may use at most 128 MiB of HBM per device.

```python
import math
import jax
import jax.numpy as jnp
from jax import lax

D = 8192
FF = 32768
TOKENS = 512


def raised(values, key, source, target, blocks, factor):
    owner, partner = [(jnp.arange(values.shape[axis_at]) // (values.shape[axis_at] // blocks)).reshape([-1 if axis == axis_at else 1 for axis in range(values.ndim)]) for axis_at in (source, target)]
    chosen = jax.random.permutation(key, blocks)[partner]
    strong = (owner == chosen) | (owner == (partner + blocks // 2) % blocks)
    return jnp.where(strong, factor * values, values)


def level_of(rng, extent, cuts, low, top_value):
    gain, own = 1.0, jax.random.fold_in(rng, 6)
    for position, blocks in cuts:
        steps = jnp.exp(jax.random.uniform(jax.random.fold_in(own, position), (blocks,), jnp.float32, low / len(cuts), top_value / len(cuts)))
        gain = gain * jnp.repeat(steps, extent[position] // blocks).reshape([-1 if axis == position else 1 for axis in range(len(extent))])
    return gain


def scatter_about(own_key, dims, width, most, cuts=(), kind=jnp.bfloat16):
    result = jax.random.normal(own_key, dims, jnp.float32) * width
    if len(cuts) > 0:
        result = level_of(own_key, dims, cuts, -0.22, 0.18) * result
    return jnp.clip(result, min=-most, max=most).astype(kind)


def bell_draw_with(stream_key, dims, scale, limit, split, heavy, dtype=jnp.bfloat16):
    array = scale * jax.random.normal(stream_key, dims, jnp.float32)
    if split:
        array = array * level_of(stream_key, dims, split, -0.22, 0.18)
    return jnp.clip(raised(array, jax.random.fold_in(stream_key, 3), *heavy), -limit, limit).astype(dtype)


def setup_inputs(seed: int = 0) -> dict:
    arg_keys = jax.random.split(jax.random.key(seed), 5)
    return {
        "tokens": bell_draw_with(arg_keys[0], (TOKENS, D), 1.0, 6.0, ((0, 4), (1, 8)), (1, 0, 8, 2.0)),
        "weight_in": scatter_about(arg_keys[1], (D, FF), D ** -0.5, 0.0625, ((0, 8), (1, 4))),
        "weight_out": scatter_about(arg_keys[2], (FF, D), FF ** -0.5, 0.03125, ((0, 4), (1, 8))),
        "upstream": bell_draw_with(arg_keys[3], (TOKENS, D), 0.25, 1.5, ((0, 4), (1, 8)), (1, 0, 8, 2.0)),
    }


def gelu_value(value):
    return 0.5 * value * (1.0 + jax.scipy.special.erf(value / math.sqrt(2.0)))

def gelu_slope(value):
    normal_part = jnp.exp(-0.5 * value * value) / math.sqrt(2.0 * math.pi)
    return 0.5 * (1.0 + jax.scipy.special.erf(value / math.sqrt(2.0))) + value * normal_part

def reference(tokens, weight_in, weight_out, upstream):
    hidden = jnp.dot(tokens, weight_in, preferred_element_type=jnp.float32)
    act = gelu_value(hidden).astype(jnp.bfloat16)
    output = jnp.dot(act, weight_out, preferred_element_type=jnp.float32).astype(jnp.bfloat16)
    grad_act = lax.dot_general(upstream, weight_out, (((1,), (1,)), ((), ())), preferred_element_type=jnp.float32)
    grad_hidden = (grad_act * gelu_slope(hidden)).astype(jnp.bfloat16)
    grad_weight_out = lax.dot_general(act, upstream, (((0,), (0,)), ((), ())), preferred_element_type=jnp.float32).astype(jnp.bfloat16)
    grad_weight_in = lax.dot_general(tokens, grad_hidden, (((0,), (0,)), ((), ())), preferred_element_type=jnp.float32).astype(jnp.bfloat16)
    grad_tokens = lax.dot_general(grad_hidden, weight_in, (((1,), (1,)), ((), ())), preferred_element_type=jnp.float32).astype(jnp.bfloat16)
    return (output, grad_tokens, grad_weight_in, grad_weight_out)
```

```python
import math

import jax
import jax.numpy as jnp
from jax import lax
from jax.sharding import PartitionSpec as P

PIECES = 4


def gelu_value(value):
    return 0.5 * value * (1.0 + jax.scipy.special.erf(value / math.sqrt(2.0)))


def gelu_slope(value):
    normal_part = jnp.exp(-0.5 * value * value) / math.sqrt(2.0 * math.pi)
    return 0.5 * (1.0 + jax.scipy.special.erf(value / math.sqrt(2.0))) + value * normal_part


def contract_last(left, right):
    return lax.dot_general(
        left, right, (((1,), (1,)), ((), ())), preferred_element_type=jnp.float32
    )


def contract_first(left, right):
    return lax.dot_general(
        left, right, (((0,), (0,)), ((), ())), preferred_element_type=jnp.float32
    )


def plain(left, right):
    return jnp.dot(left, right, preferred_element_type=jnp.float32)


def bits_of(count, piece):
    bits = []
    bit = 1
    while bit < count:
        bits.append(bit)
        bit *= 2
    chips = bits[1:]
    return bits[:1] + (chips if piece % 2 == 0 else chips[::-1])


def swap(value, count, bit):
    return lax.ppermute(value, "col", [(i, i ^ bit) for i in range(count)])


def sum_and_split(rows, weight, product, count, bits):
    half = rows.shape[0] // 2
    sent = product(rows[half:], weight).astype(jnp.bfloat16)
    kept = product(rows[:half], weight)
    total = kept + swap(sent, count, bits[0]).astype(jnp.float32)
    for bit in bits[1:]:
        half = total.shape[0] // 2
        arrived = swap(total[half:].astype(jnp.bfloat16), count, bit)
        total = total[:half] + arrived.astype(jnp.float32)
    return total


def gather_rows(block, count, bits):
    for bit in bits[::-1]:
        block = jnp.concatenate([block, swap(block, count, bit)], axis=0)
    return block


def order_of(count, bits):
    order = [0]
    for bit in bits[::-1]:
        order = order + [entry ^ bit for entry in order]
    return order


def body(tokens, weight_in, weight_out, upstream):
    count = lax.axis_size("col")
    me = lax.axis_index("col")
    gathered_tokens = lax.all_gather(tokens, "row", axis=0, tiled=True)
    gathered_upstream = lax.all_gather(upstream, "row", axis=0, tiled=True)
    all_tokens = gathered_tokens.shape[0]
    block = all_tokens // count

    def picked(rows, places):
        return jnp.concatenate(
            [lax.dynamic_slice_in_dim(rows, place * block, block, 0) for place in places], axis=0
        )

    def arranged(rows, bits):
        return picked(rows, [me ^ entry for entry in order_of(count, bits)])

    def restored(rows, bits):
        order = order_of(count, bits)
        mine = sum(((me // bit) % 2) * order.index(bit) for bit in bits)
        return picked(rows, [mine ^ order.index(i) for i in range(count)])

    orders = [bits_of(count, parity) for parity in range(2)]
    token_rows = [arranged(gathered_tokens, bits) for bits in orders]
    upstream_rows = [arranged(gathered_upstream, bits) for bits in orders]

    hidden_units = weight_in.shape[1]
    size = hidden_units // PIECES
    output_parts = [None, None]
    grad_parts = [None, None]
    hiddens = []
    grads_in = []
    grads_out = []

    def add(parts, slot, value):
        parts[slot] = value if parts[slot] is None else parts[slot] + value

    acts = []
    for piece in range(PIECES):
        slot = piece % 2
        cols = slice(piece * size, (piece + 1) * size)
        hidden = sum_and_split(
            token_rows[slot], weight_in[:, cols], plain, count, orders[slot]
        )
        hiddens.append(hidden)
        act = gather_rows(gelu_value(hidden).astype(jnp.bfloat16), count, orders[slot])
        acts.append(act)
    for piece in range(PIECES):
        slot = piece % 2
        cols = slice(piece * size, (piece + 1) * size)
        add(output_parts, slot, plain(acts[piece], weight_out[cols]))
    output = lax.psum_scatter(
        restored(output_parts[0], orders[0]) + restored(output_parts[1], orders[1]),
        "row",
        scatter_dimension=0,
        tiled=True,
    ).astype(jnp.bfloat16)

    for piece in range(PIECES):
        slot = piece % 2
        cols = slice(piece * size, (piece + 1) * size)
        grad_act = sum_and_split(
            upstream_rows[slot], weight_out[cols], contract_last, count, orders[slot]
        )
        grad_hidden = (grad_act * gelu_slope(hiddens[piece])).astype(jnp.bfloat16)
        grad_hidden = gather_rows(grad_hidden, count, orders[slot])
        grads_out.append(
            contract_first(acts[piece], upstream_rows[slot]).astype(jnp.bfloat16)
        )
        grads_in.append(
            contract_first(token_rows[slot], grad_hidden).astype(jnp.bfloat16)
        )
        add(grad_parts, slot, contract_last(grad_hidden, weight_in[:, cols]))
    grad_tokens = lax.psum_scatter(
        restored(grad_parts[0], orders[0]) + restored(grad_parts[1], orders[1]),
        "row",
        scatter_dimension=0,
        tiled=True,
    ).astype(jnp.bfloat16)
    grad_weight_in = jnp.concatenate(grads_in, axis=1)
    grad_weight_out = jnp.concatenate(grads_out, axis=0)
    return (output, grad_tokens, grad_weight_in, grad_weight_out)


def solution(mesh):
    return jax.shard_map(
        body,
        mesh=mesh,
        in_specs=(P("row", "col"), P("col", "row"), P("row", "col"), P("row", "col")),
        out_specs=(P("row", "col"), P("row", "col"), P("col", "row"), P("row", "col")),
        check_vma=False,
    )
```

```python
import math

import jax
import jax.numpy as jnp
from jax import lax
from jax.sharding import PartitionSpec as P

PIECES = 4


def gelu_value(value):
    return 0.5 * value * (1.0 + jax.scipy.special.erf(value / math.sqrt(2.0)))


def gelu_slope(value):
    normal_part = jnp.exp(-0.5 * value * value) / math.sqrt(2.0 * math.pi)
    return 0.5 * (1.0 + jax.scipy.special.erf(value / math.sqrt(2.0))) + value * normal_part


def contract_last(left, right):
    return lax.dot_general(
        left, right, (((1,), (1,)), ((), ())), preferred_element_type=jnp.float32
    )


def contract_first(left, right):
    return lax.dot_general(
        left, right, (((0,), (0,)), ((), ())), preferred_element_type=jnp.float32
    )


def plain(left, right):
    return jnp.dot(left, right, preferred_element_type=jnp.float32)


def bits_of(count, piece):
    bits = []
    bit = 1
    while bit < count:
        bits.append(bit)
        bit *= 2
    chips = bits[1:]
    return bits[:1] + (chips if piece % 2 == 0 else chips[::-1])


def swap(value, count, bit):
    return lax.ppermute(value, "col", [(i, i ^ bit) for i in range(count)])


def sum_and_split(rows, weight, product, count, bits):
    half = rows.shape[0] // 2
    sent = product(rows[half:], weight).astype(jnp.bfloat16)
    kept = product(rows[:half], weight)
    total = kept + swap(sent, count, bits[0]).astype(jnp.float32)
    for bit in bits[1:]:
        half = total.shape[0] // 2
        arrived = swap(total[half:].astype(jnp.bfloat16), count, bit)
        total = total[:half] + arrived.astype(jnp.float32)
    return total


def gather_rows(block, count, bits):
    for bit in bits[::-1]:
        block = jnp.concatenate([block, swap(block, count, bit)], axis=0)
    return block


def order_of(count, bits):
    order = [0]
    for bit in bits[::-1]:
        order = order + [entry ^ bit for entry in order]
    return order


def body(tokens, weight_in, weight_out, upstream):
    count = lax.axis_size("col")
    me = lax.axis_index("col")
    row_count = lax.axis_size("row")
    row_me = lax.axis_index("row")
    own_rows = tokens.shape[0]
    all_tokens = own_rows * row_count

    def from_rows(value):
        arrived = [
            lax.ppermute(value, "row", [(i, (i + k) % row_count) for i in range(row_count)])
            for k in range(1, row_count)
        ]
        return jnp.concatenate([value] + arrived, axis=0)

    gathered_tokens = from_rows(tokens)
    upstream, gathered_tokens = lax.optimization_barrier((upstream, gathered_tokens))
    gathered_upstream = from_rows(upstream)
    block = all_tokens // count

    def picked(rows, places):
        return jnp.concatenate(
            [lax.dynamic_slice_in_dim(rows, place * block, block, 0) for place in places], axis=0
        )

    def arranged(rows, bits):
        starts = [(me ^ entry) * block for entry in order_of(count, bits)]
        starts = [
            ((row_me - start // own_rows + row_count) % row_count) * own_rows + start % own_rows
            for start in starts
        ]
        return picked(rows, [start // block for start in starts])

    def restored(rows, bits):
        order = order_of(count, bits)
        mine = sum(((me // bit) % 2) * order.index(bit) for bit in bits)
        return picked(rows, [mine ^ order.index(i) for i in range(count)])

    orders = [bits_of(count, parity) for parity in range(2)]
    token_rows = [arranged(gathered_tokens, bits) for bits in orders]

    hidden_units = weight_in.shape[1]
    size = hidden_units // PIECES
    output_parts = [None, None]
    grad_parts = [None, None]
    hiddens = []
    grads_in = []
    grads_out = []

    def add(parts, slot, value):
        parts[slot] = value if parts[slot] is None else parts[slot] + value

    acts = []
    for piece in range(PIECES):
        slot = piece % 2
        cols = slice(piece * size, (piece + 1) * size)
        hidden = sum_and_split(
            token_rows[slot], weight_in[:, cols], plain, count, orders[slot]
        )
        hiddens.append(hidden)
    gathered_upstream, hiddens[-1] = lax.optimization_barrier((gathered_upstream, hiddens[-1]))
    upstream_rows = [arranged(gathered_upstream, bits) for bits in orders]
    for piece in range(PIECES):
        slot = piece % 2
        hidden = hiddens[piece]
        act = gather_rows(gelu_value(hidden).astype(jnp.bfloat16), count, orders[slot])
        acts.append(act)
    for piece in range(PIECES):
        slot = piece % 2
        cols = slice(piece * size, (piece + 1) * size)
        add(output_parts, slot, plain(acts[piece], weight_out[cols]))
    output = lax.psum_scatter(
        restored(output_parts[0], orders[0]) + restored(output_parts[1], orders[1]),
        "row",
        scatter_dimension=0,
        tiled=True,
    ).astype(jnp.bfloat16)

    for piece in range(PIECES):
        slot = piece % 2
        cols = slice(piece * size, (piece + 1) * size)
        grad_act = sum_and_split(
            upstream_rows[slot], weight_out[cols], contract_last, count, orders[slot]
        )
        grad_hidden = (grad_act * gelu_slope(hiddens[piece])).astype(jnp.bfloat16)
        grad_hidden = gather_rows(grad_hidden, count, orders[slot])
        grads_out.append(
            contract_first(acts[piece], upstream_rows[slot]).astype(jnp.bfloat16)
        )
        grads_in.append(
            contract_first(token_rows[slot], grad_hidden).astype(jnp.bfloat16)
        )
        add(grad_parts, slot, contract_last(grad_hidden, weight_in[:, cols]))
    grad_tokens = lax.psum_scatter(
        restored(grad_parts[0], orders[0]) + restored(grad_parts[1], orders[1]),
        "row",
        scatter_dimension=0,
        tiled=True,
    ).astype(jnp.bfloat16)
    grad_weight_in = jnp.concatenate(grads_in, axis=1)
    grad_weight_out = jnp.concatenate(grads_out, axis=0)
    return (output, grad_tokens, grad_weight_in, grad_weight_out)


def solution(mesh):
    return jax.shard_map(
        body,
        mesh=mesh,
        in_specs=(P("row", "col"), P("col", "row"), P("row", "col"), P("row", "col")),
        out_specs=(P("row", "col"), P("row", "col"), P("col", "row"), P("row", "col")),
        check_vma=False,
    )
```
